256 devices in a mesh: hst: 16 (over z_lo, x), dev: 16 (over y, z_hi, core).
Axes of the slice: x: 4, y: 4, z: 8 (z_hi: 2, z_lo: 4; z = z_hi * 4 + z_lo), core: 2. Of those that a mesh axis runs over, the one named last changes fastest.
Arguments:
- grad_out: bfloat16 [32768, 6144], P(('hst', 'dev')), may hold values from -6 to 6
- gates: float32 [32768], P(('hst', 'dev')), may hold values from 0.1 to 1
- route_rows: int32 [8704], P(('hst', 'dev')), may hold values from 0 to 128, as said below
- saved_act: bfloat16 [8704, 8192], P(('hst', 'dev')), may hold values from -6 to 6
- queries: bfloat16 [32768, 768], P(('hst', 'dev')), may hold values from -64 to 64
- keys: bfloat16 [32768, 128], P(('hst', 'dev')), may hold values from -16 to 16
- values: bfloat16 [32768, 128], P(('hst', 'dev')), may hold values from -6 to 6
- out_proj: bfloat16 [768, 6144], P(None, 'dev'), may hold values from -0.21875 to 0.21875
- w_down: bfloat16 [6144, 8192], P(None, 'dev'), may hold values from -0.0625 to 0.0625
Outputs:
- act_grad: bfloat16 [8704, 8192], P(('hst', 'dev'))
- query_grad: bfloat16 [32768, 768], P(('hst', 'dev'))
- key_grad: bfloat16 [32768, 128], P(('hst', 'dev'))
- value_grad: bfloat16 [32768, 128], P(('hst', 'dev'))
- proj_grad: float32 [768, 6144], P('hst', 'dev')
- down_grad: float32 [6144, 8192], P('hst', 'dev')
The draws below stay inside these ranges and needn't reach their ends.
Inputs may be any that keep to these rules, and one draw needn't show every extreme that they name: `route_rows`: each block's 34 entries list distinct rows below 128 in increasing order, then 128 for the empty slots. At least half of every block's slots are used, and in some sequence every block uses all 34.
All inputs are finite; a program needn't handle non-finite values.
Results may differ from the reference program's by a relative error of at most 0.024.
Values may be sent and summed in bfloat16 or wider, within the bound.
No kernel may reach another device: no remote copies, remote signals or barrier semaphores. Data moves between devices by JAX's collectives and lax.ppermute only.
A program may use at most 128 MiB of HBM per device.

```python
import math
import jax
import jax.numpy as jnp
from jax import lax

D = 6144
HEAD = 128
FF_WIN = 8192
TOK_DEV = 128
ATT = 768
MOST = 34
SEQ = 2048
TOKENS = 32768
SLOTS = 8704
N_HST = 16
N_DEV = 16


def draw_queries(key, part):
    key = jax.random.fold_in(key, 3)
    result = jnp.clip(jax.random.normal(key, (TOKENS, ATT), jnp.float32), -6.0, 6.0)
    return result.astype(jnp.bfloat16)


def draw_keys(key, part):
    key = jax.random.fold_in(key, 4)
    result = jnp.clip(jax.random.normal(key, (TOKENS, HEAD), jnp.float32), -6.0, 6.0)
    return result.astype(jnp.bfloat16)


def draw_route_rows(key, part):
    key = jax.random.fold_in(key, 7)
    blocks = TOKENS // TOK_DEV
    per_sequence = SEQ // TOK_DEV
    count_key, full_key, order_key = jax.random.split(key, 3)
    counts = jax.random.randint(count_key, (blocks,), MOST // 2, MOST + 1)
    full_sequence = jax.random.randint(full_key, (), 0, blocks // per_sequence)
    counts = jnp.where(jnp.arange(blocks) // per_sequence == full_sequence, MOST, counts)
    order_keys = jax.random.split(order_key, blocks)
    orders = jax.vmap(lambda one: jax.random.permutation(one, TOK_DEV))(order_keys)[:, :MOST]
    chosen = jnp.where(jnp.arange(MOST)[None, :] < counts[:, None], orders, TOK_DEV)
    chosen = jnp.sort(chosen, axis=1)
    return chosen.reshape(-1).astype(jnp.int32)


def level_of(stream_key, extent, cuts, low, high):
    factor_of, own = 1.0, jax.random.fold_in(stream_key, 6)
    for dim, shards_of in cuts:
        steps = jnp.exp(jax.random.uniform(jax.random.fold_in(own, dim), (shards_of,), jnp.float32, low / len(cuts), high / len(cuts)))
        factor_of = factor_of * jnp.repeat(steps, extent[dim] // shards_of).reshape([-1 if axis == dim else 1 for axis in range(len(extent))])
    return factor_of


def bell_draw(key, dims, deviation, most, shards=(), kind=jnp.bfloat16):
    gain = level_of(key, dims, shards, -0.22, 0.18) if shards else 1.0
    entries = jax.random.normal(key, dims, jnp.float32) * deviation * gain
    return jnp.minimum(jnp.maximum(entries, -most), most).astype(kind)


def setup_inputs(seed: int = 0) -> dict:
    splits = jax.random.split(jax.random.key(seed), 10)
    return {
        "grad_out": bell_draw(splits[0], (TOKENS, D), 1.0, 6.0, ((0, 256),)),
        "gates": jnp.clip(jnp.exp(math.log(1.0) - 2.3025851 * jax.random.uniform(splits[1], (TOKENS,), jnp.float32) ** level_of(splits[1], (TOKENS,), ((0, 256),), -0.2, 0.2)), 0.1, 1.0),
        "route_rows": draw_route_rows(jax.random.fold_in(splits[9], 71), 0),
        "saved_act": bell_draw(splits[3], (SLOTS, FF_WIN), 1.0, 6.0, ((0, 256),)),
        "queries": draw_queries(jax.random.fold_in(splits[9], 71), 0),
        "keys": draw_keys(jax.random.fold_in(splits[9], 71), 0),
        "values": bell_draw(splits[6], (TOKENS, HEAD), 1.0, 6.0, ((0, 256),)),
        "out_proj": bell_draw(splits[7], (ATT, D), ATT ** -0.5, 0.21875, ((1, 16),)),
        "w_down": bell_draw(splits[8], (D, FF_WIN), FF_WIN ** -0.5, 0.0625, ((1, 16),)),
    }


def reference(grad_out, gates, route_rows, saved_act, queries, keys, values, out_proj, w_down):
    sequence_len = TOK_DEV * N_DEV
    slot_len = MOST * N_DEV
    head_count = ATT // HEAD
    score_scale = HEAD ** -0.5
    positions = jnp.arange(sequence_len)
    allowed = positions[None, :] <= positions[:, None]
    slot_block = (jnp.arange(slot_len) // MOST).astype(jnp.int32)

    def host_pass(carry, host):
        start = (host * sequence_len).astype(jnp.int32)
        slot_start = (host * slot_len).astype(jnp.int32)
        host_grad = lax.dynamic_slice_in_dim(grad_out, start, sequence_len, 0)
        host_gates = lax.dynamic_slice_in_dim(gates, start, sequence_len, 0)
        host_routes = lax.dynamic_slice_in_dim(route_rows, slot_start, slot_len, 0)
        host_act = lax.dynamic_slice_in_dim(saved_act, slot_start, slot_len, 0)
        query_rows = lax.dynamic_slice_in_dim(queries, start, sequence_len, 0)
        key_rows = lax.dynamic_slice_in_dim(keys, start, sequence_len, 0)
        value_rows = lax.dynamic_slice_in_dim(values, start, sequence_len, 0)
        token_index = jnp.where(host_routes < TOK_DEV, slot_block * TOK_DEV + host_routes,
                                sequence_len).astype(jnp.int32)
        padded_grad = jnp.concatenate([host_grad, jnp.zeros((1, D), jnp.bfloat16)], 0)
        padded_gate = jnp.concatenate([host_gates, jnp.zeros((1,), jnp.float32)], 0)
        upstream = (padded_gate[token_index][:, None] * padded_grad[token_index].astype(jnp.float32)).astype(jnp.bfloat16)
        act_grad = jnp.dot(upstream, w_down, preferred_element_type=jnp.float32).astype(jnp.bfloat16)
        down_part = jnp.dot(upstream.T, host_act, preferred_element_type=jnp.float32).astype(jnp.bfloat16)

        query3 = query_rows.reshape(sequence_len, head_count, HEAD).astype(jnp.float32)
        key_f = key_rows.astype(jnp.float32)
        value_f = value_rows.astype(jnp.float32)
        scores = jnp.einsum("qhd,kd->hqk", query3, key_f) * score_scale
        scores = jnp.where(allowed[None], scores, jnp.float32(-1e30))
        highest = jnp.max(scores, axis=2, keepdims=True)
        weights = jnp.exp(scores - highest)
        probs = weights / jnp.sum(weights, axis=2, keepdims=True)
        probs_b = probs.astype(jnp.bfloat16)
        attended = jnp.einsum("hqk,kd->qhd", probs_b.astype(jnp.float32), value_f).astype(jnp.bfloat16)
        attended_flat = attended.reshape(sequence_len, ATT)
        attn_grad = jnp.dot(host_grad, out_proj.T, preferred_element_type=jnp.float32).astype(jnp.bfloat16)
        proj_part = jnp.dot(attended_flat.T, host_grad, preferred_element_type=jnp.float32).astype(jnp.bfloat16)
        attn_grad3 = attn_grad.reshape(sequence_len, head_count, HEAD).astype(jnp.float32)
        prob_grad = jnp.einsum("qhd,kd->hqk", attn_grad3, value_f)
        row_dot = jnp.sum(attn_grad3 * attended.astype(jnp.float32), axis=2)
        score_grad = (probs * (prob_grad - row_dot.T[:, :, None])).astype(jnp.bfloat16)
        score_f = score_grad.astype(jnp.float32)
        query_grad = (jnp.einsum("hqk,kd->qhd", score_f, key_f) * score_scale).astype(jnp.bfloat16)
        key_grad = (jnp.einsum("hqk,qhd->kd", score_f, query3) * score_scale).astype(jnp.bfloat16)
        value_grad = jnp.einsum("hqk,qhd->kd", probs_b.astype(jnp.float32), attn_grad3).astype(jnp.bfloat16)
        proj_sum, down_sum = carry
        carry = (proj_sum + proj_part.astype(jnp.float32), down_sum + down_part.astype(jnp.float32))
        return carry, (act_grad, query_grad.reshape(sequence_len, ATT), key_grad, value_grad)

    start_carry = (jnp.zeros((ATT, D), jnp.float32), jnp.zeros((D, FF_WIN), jnp.float32))
    sums, outputs = lax.scan(host_pass, start_carry, jnp.arange(N_HST, dtype=jnp.int32))
    act_grad = outputs[0].reshape(SLOTS, FF_WIN)
    query_grad = outputs[1].reshape(TOKENS, ATT)
    key_grad = outputs[2].reshape(TOKENS, HEAD)
    value_grad = outputs[3].reshape(TOKENS, HEAD)
    return act_grad, query_grad, key_grad, value_grad, sums[0], sums[1]
```

```python
import jax
import jax.numpy as jnp
from jax import lax
from jax.sharding import Mesh, PartitionSpec as P

HEAD = 128
SLOT_PAD = 40
F32 = jnp.float32
BF16 = jnp.bfloat16


def shift(value, axis, by):
    size = lax.axis_size(axis)
    return lax.ppermute(value, axis, [(i, (i + by) % size) for i in range(size)])


def add32(*terms):
    total = terms[0].astype(F32)
    for term in terms[1:]:
        total = total + term.astype(F32)
    return total


def ring_pieces(value):
    return [value, shift(value, "y", -1), shift(value, "y", 2), shift(value, "y", 1)]


def pick(array, index):
    return lax.dynamic_index_in_dim(array, index, 0, keepdims=False)


def on_device(grad_out, gates, route_rows, saved_act, queries, keys, values, out_proj, w_down):
    y, zh, core = lax.axis_index("y"), lax.axis_index("zh"), lax.axis_index("core")
    tokens, width = grad_out.shape
    slots = route_rows.shape[0]
    heads = queries.shape[1] // HEAD
    cols = out_proj.shape[1]
    hidden = w_down.shape[1]
    scale = HEAD ** (-0.5)
    contract_rows = (((0,), (0,)), ((), ()))
    contract_cols = (((1,), (1,)), ((), ()))

    rows = jnp.concatenate([route_rows, jnp.full((SLOT_PAD - slots,), tokens, jnp.int32)])
    hot = rows[:, None] == jnp.arange(tokens, dtype=jnp.int32)[None, :]
    picked = jnp.dot(hot.astype(BF16), grad_out, preferred_element_type=F32)
    gate = jnp.sum(jnp.where(hot, gates[None, :], 0.0), axis=1)
    upstream = (gate[:, None] * picked).astype(BF16)

    other_up = shift(upstream, "zh", 1)
    near = jnp.concatenate(ring_pieces(upstream), 0)
    far = jnp.concatenate(ring_pieces(other_up), 0)
    near_core = shift(near, "core", 1)
    far_core = shift(far, "core", 1)
    piece = jnp.concatenate([near, far, near_core, far_core], 0)

    order = [(f, e, d) for f in range(2) for e in range(2) for d in range(4)]
    act_in = jnp.concatenate([saved_act, jnp.zeros((SLOT_PAD - slots, saved_act.shape[1]), BF16)], 0)
    act_in = act_in.reshape(SLOT_PAD, 16, hidden).transpose(1, 0, 2)
    act_all = lax.all_to_all(act_in, ("y", "zh", "core"), 0, 0, tiled=True)
    act_rel = jnp.concatenate(
        [pick(act_all, ((y + d) % 4) * 4 + (zh ^ e) * 2 + (core ^ f)) for f, e, d in order], 0
    )
    down = lax.dot_general(piece, act_rel, contract_rows, preferred_element_type=F32).astype(BF16)
    down_grad = lax.psum_scatter(down, ("zl", "x"), scatter_dimension=0, tiled=True).astype(F32)

    part = jnp.dot(piece, w_down, preferred_element_type=F32).astype(BF16)
    part = part.reshape(16, SLOT_PAD, hidden)
    back = []
    for place in range(16):
        py, pz, pc = place // 4, (place // 2) % 2, place % 2
        back.append(pick(part, (core ^ pc) * 8 + (zh ^ pz) * 4 + (py - y) % 4))
    act_back = lax.all_to_all(jnp.stack(back), ("y", "zh", "core"), 0, 0, tiled=True)
    act_grad = act_back.transpose(1, 0, 2).reshape(SLOT_PAD, 16 * hidden)[:slots]

    kv = jnp.concatenate([keys, values], 1)
    kv2 = jnp.stack([kv, shift(kv, "zh", 1)])
    kv8 = jnp.stack(ring_pieces(kv2))
    kv16 = jnp.stack([kv8, shift(kv8, "core", 1)])
    all_kv = kv16.reshape(16 * tokens, 2 * HEAD)
    all_keys, all_values = all_kv[:, :HEAD], all_kv[:, HEAD:]
    place = jnp.arange(16, dtype=jnp.int32)
    block = ((y + (place // 2) % 4) % 4) * 4 + (zh ^ (place % 2)) * 2 + (core ^ (place // 8))
    key_place = (block[:, None] * tokens + jnp.arange(tokens, dtype=jnp.int32)[None, :]).reshape(-1)
    query_place = (y * 4 + zh * 2 + core) * tokens + jnp.arange(tokens, dtype=jnp.int32)

    query3 = queries.reshape(tokens, heads, HEAD)
    scores = jnp.einsum("qhd,kd->hqk", query3, all_keys, preferred_element_type=F32) * scale
    allowed = key_place[None, :] <= query_place[:, None]
    scores = jnp.where(allowed[None], scores, jnp.float32(-1e30))
    highest = jnp.max(scores, axis=2, keepdims=True)
    weights = jnp.exp(scores - highest)
    probs = weights / jnp.sum(weights, axis=2, keepdims=True)
    probs_b = probs.astype(BF16)
    attended = jnp.einsum("hqk,kd->qhd", probs_b, all_values, preferred_element_type=F32).astype(BF16)

    cols_in = grad_out.reshape(tokens, 4, 2, 2, cols).transpose(1, 3, 0, 2, 4)
    cols_in = cols_in.reshape(8, tokens, 2 * cols)
    cols_all = lax.all_to_all(cols_in, ("y", "core"), 0, 0, tiled=True).reshape(8 * tokens, 2 * cols)

    other_proj = shift(out_proj, "zh", 1)
    first = zh == 0
    both_proj = jnp.concatenate(
        [jnp.where(first, out_proj, other_proj), jnp.where(first, other_proj, out_proj)], 1
    )
    grad_part = lax.dot_general(cols_all, both_proj, contract_cols, preferred_element_type=F32)
    grad_part = grad_part.astype(BF16).reshape(4, 2, tokens, heads * HEAD)
    mine = lax.dynamic_index_in_dim(grad_part, core, 1, keepdims=False)
    theirs = lax.dynamic_index_in_dim(grad_part, 1 - core, 1, keepdims=False)
    chip_sum = add32(mine, shift(theirs, "core", 1)).astype(BF16)
    attn_grad = add32(
        pick(chip_sum, y),
        *[shift(pick(chip_sum, (y + d) % 4), "y", d) for d in (1, 2, 3)],
    ).astype(BF16)

    flat = attended.reshape(tokens, heads * HEAD)
    att4 = jnp.stack(ring_pieces(flat))
    att8 = jnp.stack([att4, shift(att4, "core", 1)]).reshape(8, tokens, heads * HEAD)
    att_all = jnp.concatenate(
        [pick(att8, (core ^ (p % 2)) * 4 + (p // 2 - y) % 4) for p in range(8)], 0
    )
    proj = lax.dot_general(att_all, cols_all, contract_rows, preferred_element_type=F32).astype(BF16)
    proj_rows = proj.shape[0] // 16
    proj16 = lax.all_to_all(proj.reshape(16, proj_rows, 2 * cols), ("zl", "x"), 0, 0, tiled=True)
    proj_sum = jnp.sum(proj16.astype(F32), axis=0)
    left, right = proj_sum[:, :cols], proj_sum[:, cols:]
    keep = jnp.where(first, left, right)
    give = jnp.where(first, right, left).astype(BF16)
    proj_grad = keep + shift(give, "zh", 1).astype(F32)

    attn_grad3 = attn_grad.reshape(tokens, heads, HEAD)
    prob_grad = jnp.einsum("qhd,kd->hqk", attn_grad3, all_values, preferred_element_type=F32)
    row_dot = jnp.sum(attn_grad3.astype(F32) * attended.astype(F32), axis=2)
    score_grad = (probs * (prob_grad - row_dot.T[:, :, None])).astype(BF16)
    query_grad = jnp.einsum("hqk,kd->qhd", score_grad, all_keys, preferred_element_type=F32) * scale
    query_grad = query_grad.astype(BF16).reshape(tokens, heads * HEAD)
    key_part = jnp.einsum("hqk,qhd->kd", score_grad, query3, preferred_element_type=F32) * scale
    value_part = jnp.einsum("hqk,qhd->kd", probs_b, attn_grad3, preferred_element_type=F32)
    kv_part = jnp.concatenate([key_part, value_part], axis=1).astype(BF16)
    kv_part = kv_part.reshape(2, 4, 2, tokens, 2 * HEAD)
    kv_chip = add32(kv_part[0], shift(kv_part[1], "core", 1)).astype(BF16)
    kv_ring = add32(kv_chip[0], *[shift(kv_chip[d], "y", d) for d in (1, 2, 3)]).astype(BF16)
    kv_grad = add32(kv_ring[0], shift(kv_ring[1], "zh", 1)).astype(BF16)
    return act_grad, query_grad, kv_grad[:, :HEAD], kv_grad[:, HEAD:], proj_grad, down_grad


def solution(mesh):
    axes = ("zl", "x", "y", "zh", "core")
    fine = Mesh(mesh.devices.reshape(4, 4, 4, 2, 2), axes)
    by_token = P(axes, None)
    by_dev = P(None, ("y", "zh", "core"))
    both = P(("zl", "x"), ("y", "zh", "core"))
    return jax.shard_map(
        on_device,
        mesh=fine,
        in_specs=(by_token, P(axes), P(axes), by_token, by_token, by_token, by_token, by_dev, by_dev),
        out_specs=(by_token, by_token, by_token, by_token, both, both),
        check_vma=False,
    )
```

```python
import jax
import jax.numpy as jnp
from jax import lax
from jax.experimental import pallas as pl
from jax.experimental.pallas import tpu as pltpu
from jax.sharding import Mesh, PartitionSpec as P

HEAD = 128
SLOT_PAD = 40
F32 = jnp.float32
BF16 = jnp.bfloat16


def shift(value, axis, by):
    size = lax.axis_size(axis)
    return lax.ppermute(value, axis, [(i, (i + by) % size) for i in range(size)])


def add32(*terms):
    total = terms[0].astype(F32)
    for term in terms[1:]:
        total = total + term.astype(F32)
    return total


CHIPS = ("y", "core")
GROUP = ("y", "zh", "core")
SEQUENCES = ("zl", "x")


def swap(value, axes):
    return lax.all_to_all(value, axes, 0, 0, tiled=True)


def meet(*values):
    return lax.optimization_barrier(values)


def ring_pieces(value):
    return [value, shift(value, "y", -1), shift(value, "y", 2), shift(value, "y", 1)]


def pick(array, index):
    return lax.dynamic_index_in_dim(array, index, 0, keepdims=False)


def join_rows(joined, pieces):
    start = 0
    for piece in pieces:
        joined[start : start + piece.shape[0], :] = piece[...]
        start += piece.shape[0]


def down_product(spots, pieces, act_all):
    count, rows, hidden = act_all.shape
    width = pieces[0].shape[1]
    tile = width // 8
    piece_rows = pieces[0].shape[0]

    def kernel(spots_ref, near_ref, far_ref, act_ref, out_ref, joined, acts):
        @pl.when(pl.program_id(0) == 0)
        def _():
            for i in range(count):
                acts[rows * i : rows * (i + 1), :] = act_ref[spots_ref[i]]

        join_rows(joined, (near_ref, far_ref))
        out_ref[...] = lax.dot_general(
            joined[...], acts[...], (((0,), (0,)), ((), ())), preferred_element_type=F32
        ).astype(BF16)

    return pl.pallas_call(
        kernel,
        grid_spec=pltpu.PrefetchScalarGridSpec(
            num_scalar_prefetch=1,
            grid=(8,),
            in_specs=[pl.BlockSpec((piece_rows, tile), lambda i, s: (0, i))] * 2
            + [pl.BlockSpec((count, rows, hidden), lambda i, s: (0, 0, 0))],
            out_specs=pl.BlockSpec((tile, hidden), lambda i, s: (i, 0)),
            scratch_shapes=[pltpu.VMEM((count * rows, tile), BF16), pltpu.VMEM((count * rows, hidden), BF16)],
        ),
        out_shape=jax.ShapeDtypeStruct((width, hidden), BF16),
        compiler_params=pltpu.CompilerParams(vmem_limit_bytes=60 * 2**20),
        cost_estimate=pl.CostEstimate(
            flops=2 * count * rows * width * hidden, bytes_accessed=16 * 2**20, transcendentals=0
        ),
    )(spots, *pieces, act_all)


def act_product(spots, pieces, w_down):
    rows, held = SLOT_PAD, len(pieces)
    count = sum(p.shape[0] for p in pieces) // rows
    width, hidden = w_down.shape
    steps = 4
    tile = width // steps

    def kernel(spots_ref, *refs):
        w_ref, out_ref, joined, total = refs[held:]
        step = pl.program_id(0)
        join_rows(joined, refs[:held])
        term = jnp.dot(joined[...], w_ref[...], preferred_element_type=F32)

        @pl.when(step == 0)
        def _():
            total[...] = term

        @pl.when(step > 0)
        def _():
            total[...] += term

        @pl.when(step == steps - 1)
        def _():
            for i in range(count):
                out_ref[spots_ref[i]] = total[rows * i : rows * (i + 1), :].astype(BF16)

    return pl.pallas_call(
        kernel,
        grid_spec=pltpu.PrefetchScalarGridSpec(
            num_scalar_prefetch=1,
            grid=(steps,),
            in_specs=[pl.BlockSpec((p.shape[0], tile), lambda i, s: (0, i)) for p in pieces]
            + [pl.BlockSpec((tile, hidden), lambda i, s: (i, 0))],
            out_specs=pl.BlockSpec((count, rows, hidden), lambda i, s: (0, 0, 0)),
            scratch_shapes=[pltpu.VMEM((count * rows, tile), BF16), pltpu.VMEM((count * rows, hidden), F32)],
        ),
        out_shape=jax.ShapeDtypeStruct((count, rows, hidden), BF16),
        compiler_params=pltpu.CompilerParams(vmem_limit_bytes=60 * 2**20),
        cost_estimate=pl.CostEstimate(
            flops=2 * count * rows * width * hidden, bytes_accessed=16 * 2**20, transcendentals=0
        ),
    )(spots, *pieces, w_down)


def over_zl(mine):
    zl = lax.axis_index("zl")
    return add32(pick(mine, zl), *[shift(pick(mine, (zl + e) % 4), "zl", e) for e in (1, 2, 3)])


def attn_product(where, cols_all, out_proj, other_proj):
    _, tokens, both = cols_all.shape
    features, cols = out_proj.shape

    def kernel(where_ref, *refs):
        col_refs, own_ref, other_ref, mine_ref, theirs_ref, joined = refs[:4], *refs[4:]
        for d in range(4):
            joined[tokens * d : tokens * (d + 1), :] = col_refs[d][0]
        near = pl.multiple_of(where_ref[2] * cols, 128)
        far = pl.multiple_of((1 - where_ref[2]) * cols, 128)
        by_cols = (((1,), (1,)), ((), ()))
        product = lax.dot_general(
            joined[:, pl.ds(near, cols)], own_ref[...], by_cols, preferred_element_type=F32
        ) + lax.dot_general(joined[:, pl.ds(far, cols)], other_ref[...], by_cols, preferred_element_type=F32)
        product = product.astype(BF16).reshape(4, tokens, features)

        @pl.when(pl.program_id(0) == 0)
        def _():
            theirs_ref[...] = product

        @pl.when(pl.program_id(0) == 1)
        def _():
            mine_ref[...] = product

    def spot(d):
        return lambda i, s: (((s[0] + d) % 4) * 2 + (s[1] + 1 - i) % 2, 0, 0)

    whole = pl.BlockSpec((features, cols), lambda i, s: (0, 0))
    out = pl.BlockSpec((4, tokens, features), lambda i, s: (0, 0, 0))
    return pl.pallas_call(
        kernel,
        grid_spec=pltpu.PrefetchScalarGridSpec(
            num_scalar_prefetch=1,
            grid=(2,),
            in_specs=[pl.BlockSpec((1, tokens, both), spot(d)) for d in range(4)] + [whole, whole],
            out_specs=[out, out],
            scratch_shapes=[pltpu.VMEM((4 * tokens, both), BF16)],
        ),
        out_shape=[jax.ShapeDtypeStruct((4, tokens, features), BF16)] * 2,
        compiler_params=pltpu.CompilerParams(vmem_limit_bytes=48 * 2**20),
        cost_estimate=pl.CostEstimate(
            flops=16 * tokens * both * features, bytes_accessed=6 * 2**20, transcendentals=0
        ),
    )(where, *[cols_all] * 4, out_proj, other_proj)


def proj_product(where, mine, partner, cols_all):
    _, tokens, features = mine.shape
    both = cols_all.shape[2]

    rows = features // 16

    def kernel(where_ref, mine_ref, partner_ref, cols_ref, *refs):
        outs, (joined, sides, product) = refs[:4], refs[4:]
        for d in range(4):
            row = lax.rem(where_ref[0] + d, 4) * 2
            for f, ref in ((0, mine_ref), (1, partner_ref)):
                start = tokens * (2 * d + f)
                joined[start : start + tokens, :] = ref[d]
                sides[start : start + tokens, :] = cols_ref[row + lax.rem(where_ref[1] + f, 2)]
        product[...] = lax.dot_general(
            joined[...], sides[...], (((0,), (0,)), ((), ())), preferred_element_type=F32
        )
        for d in range(4):
            column = lax.rem(where_ref[3] + d, 4)
            for z in range(4):
                start = pl.multiple_of((4 * z + column) * rows, 16)
                outs[d][z] = product[pl.ds(start, rows), :].astype(BF16)

    piece = pl.BlockSpec((4, rows, both), lambda i, s: (0, 0, 0))
    whole = pl.BlockSpec((4, tokens, features), lambda i, s: (0, 0, 0))
    return pl.pallas_call(
        kernel,
        grid_spec=pltpu.PrefetchScalarGridSpec(
            num_scalar_prefetch=1,
            grid=(1,),
            in_specs=[whole, whole, pl.BlockSpec((8, tokens, both), lambda i, s: (0, 0, 0))],
            out_specs=[piece] * 4,
            scratch_shapes=[
                pltpu.VMEM((8 * tokens, features), BF16),
                pltpu.VMEM((8 * tokens, both), BF16),
                pltpu.VMEM((features, both), F32),
            ],
        ),
        out_shape=[jax.ShapeDtypeStruct((4, rows, both), BF16)] * 4,
        compiler_params=pltpu.CompilerParams(vmem_limit_bytes=48 * 2**20),
        cost_estimate=pl.CostEstimate(
            flops=16 * tokens * both * features, bytes_accessed=6 * 2**20, transcendentals=0
        ),
    )(where, mine, partner, cols_all)


def on_device(grad_out, gates, route_rows, saved_act, queries, keys, values, out_proj, w_down):
    y, zh, core = lax.axis_index("y"), lax.axis_index("zh"), lax.axis_index("core")
    tokens, width = grad_out.shape
    slots = route_rows.shape[0]
    heads = queries.shape[1] // HEAD
    cols = out_proj.shape[1]
    hidden = w_down.shape[1]
    scale = HEAD ** (-0.5)

    kv = jnp.concatenate([keys, values], 1)
    kv_other = shift(kv, "zh", 1)

    rows = jnp.concatenate([route_rows, jnp.full((SLOT_PAD - slots,), tokens, jnp.int32)])
    hot = rows[:, None] == jnp.arange(tokens, dtype=jnp.int32)[None, :]
    picked = jnp.dot(hot.astype(BF16), grad_out, preferred_element_type=F32)
    gate = jnp.sum(jnp.where(hot, gates[None, :], 0.0), axis=1)
    upstream = (gate[:, None] * picked).astype(BF16)

    kv2 = jnp.stack([kv, kv_other])
    kv8 = jnp.stack(ring_pieces(kv2))
    all_kv = jnp.stack([kv8, shift(kv8, "core", 1)]).reshape(16 * tokens, 2 * HEAD)
    all_keys, all_values = all_kv[:, :HEAD], all_kv[:, HEAD:]

    near = lax.all_gather(upstream, CHIPS, axis=0, tiled=True)
    upstream, kv_other = meet(upstream, kv_other)
    other_up = shift(upstream, "zh", 1)

    act_in = jnp.concatenate([saved_act, jnp.zeros((SLOT_PAD - slots, saved_act.shape[1]), BF16)], 0)
    act_in = act_in.reshape(SLOT_PAD, 16, hidden).transpose(1, 0, 2)
    cols_in = grad_out.reshape(tokens, 4, 2, 2, cols).transpose(1, 3, 0, 2, 4).reshape(8, tokens, 2 * cols)
    other_up, out_proj, act_in, cols_in = meet(other_up, out_proj, act_in, cols_in)
    far = lax.all_gather(other_up, CHIPS, axis=0, tiled=True)
    pieces = (near, far)
    spots = jnp.stack(
        [py * 4 + (zh ^ e) * 2 + pc for e in range(2) for py in range(4) for pc in range(2)]
    ).astype(jnp.int32)

    kv2 = jnp.stack([kv, kv_other])
    kv8 = jnp.stack(ring_pieces(kv2))
    all_kv = jnp.stack([kv8, shift(kv8, "core", 1)]).reshape(16 * tokens, 2 * HEAD)
    all_keys, all_values = all_kv[:, :HEAD], all_kv[:, HEAD:]

    place = jnp.arange(16, dtype=jnp.int32)
    block = ((y + (place // 2) % 4) % 4) * 4 + (zh ^ (place % 2)) * 2 + (core ^ (place // 8))
    key_place = (block[:, None] * tokens + jnp.arange(tokens, dtype=jnp.int32)[None, :]).reshape(-1)
    query_place = (y * 4 + zh * 2 + core) * tokens + jnp.arange(tokens, dtype=jnp.int32)

    query3 = queries.reshape(tokens, heads, HEAD)
    scores = jnp.einsum("qhd,kd->hqk", query3, all_keys, preferred_element_type=F32) * scale
    allowed = key_place[None, :] <= query_place[:, None]
    scores = jnp.where(allowed[None], scores, jnp.float32(-1e30))
    highest = jnp.max(scores, axis=2, keepdims=True)
    weights = jnp.exp(scores - highest)
    probs = weights / jnp.sum(weights, axis=2, keepdims=True)
    probs_b = probs.astype(BF16)
    attended = jnp.einsum("hqk,kd->qhd", probs_b, all_values, preferred_element_type=F32).astype(BF16)

    flat = attended.reshape(tokens, heads * HEAD)
    other_proj = shift(out_proj, "zh", 1)
    spots, flat, other_proj = meet(spots, flat, other_proj)
    act_all = swap(act_in, GROUP)

    where = jnp.stack([y, core, zh, lax.axis_index("x")]).astype(jnp.int32)
    down = down_product(spots, pieces, act_all)

    cols_in, spots, where, down = meet(cols_in, spots, where, down)
    down_grad = lax.psum_scatter(down, SEQUENCES, scatter_dimension=0, tiled=True).astype(F32)
    cols_all = swap(cols_in, CHIPS)

    part = act_product(spots, pieces, w_down)

    att4 = jnp.stack(ring_pieces(flat))
    att_other = shift(att4, "core", 1)
    where, part = meet(where, part)
    mine, theirs = attn_product(where, cols_all, out_proj, other_proj)
    act_back = swap(part, GROUP)
    chip_sum = add32(mine, shift(theirs, "core", 1)).astype(BF16)
    attn_grad = add32(chip_sum[0], *[shift(chip_sum[d], "y", d) for d in (1, 2, 3)]).astype(BF16)

    where, attn_grad = meet(where, attn_grad)
    proj = proj_product(where, att4, att_other, cols_all)

    attn_grad3 = attn_grad.reshape(tokens, heads, HEAD)
    prob_grad = jnp.einsum("qhd,kd->hqk", attn_grad3, all_values, preferred_element_type=F32)
    row_dot = jnp.sum(attn_grad3.astype(F32) * attended.astype(F32), axis=2)
    score_grad = (probs * (prob_grad - row_dot.T[:, :, None])).astype(BF16)
    query_grad = jnp.einsum("hqk,kd->qhd", score_grad, all_keys, preferred_element_type=F32) * scale
    query_grad = query_grad.astype(BF16).reshape(tokens, heads * HEAD)
    key_part = jnp.einsum("hqk,qhd->kd", score_grad, query3, preferred_element_type=F32) * scale
    value_part = jnp.einsum("hqk,qhd->kd", probs_b, attn_grad3, preferred_element_type=F32)
    kv_part = jnp.concatenate([key_part, value_part], axis=1).astype(BF16)
    kv_part = kv_part.reshape(2, 4, 2, tokens, 2 * HEAD)
    kv_chip = add32(kv_part[0], shift(kv_part[1], "core", 1)).astype(BF16)
    kv_ring = add32(kv_chip[0], *[shift(kv_chip[d], "y", d) for d in (1, 2, 3)]).astype(BF16)
    proj = add32(proj[0], *[shift(proj[d], "x", d) for d in (1, 2, 3)]).astype(BF16)
    act_back, proj, kv_ring = meet(act_back, proj, kv_ring)
    act_grad = act_back.transpose(1, 0, 2).reshape(SLOT_PAD, 16 * hidden)[:slots]
    proj = over_zl(proj)
    left, right = proj[:, :cols], proj[:, cols:]
    keep = jnp.where(zh == 0, left, right)
    give = jnp.where(zh == 0, right, left).astype(BF16)
    proj_grad = keep + shift(give, "zh", 1).astype(F32)

    kv_grad = add32(kv_ring[0], shift(kv_ring[1], "zh", 1)).astype(BF16)
    return act_grad, query_grad, kv_grad[:, :HEAD], kv_grad[:, HEAD:], proj_grad, down_grad


def solution(mesh):
    axes = ("zl", "x", "y", "zh", "core")
    fine = Mesh(mesh.devices.reshape(4, 4, 4, 2, 2), axes)
    by_token = P(axes, None)
    by_dev = P(None, ("y", "zh", "core"))
    both = P(("zl", "x"), ("y", "zh", "core"))
    return jax.shard_map(
        on_device,
        mesh=fine,
        in_specs=(by_token, P(axes), P(axes), by_token, by_token, by_token, by_token, by_dev, by_dev),
        out_specs=(by_token, by_token, by_token, by_token, both, both),
        check_vma=False,
    )
```

```python
import jax
import jax.numpy as jnp
from jax import lax
from jax.experimental import pallas as pl
from jax.experimental.pallas import tpu as pltpu
from jax.sharding import Mesh, PartitionSpec as P

HEAD = 128
SLOT_PAD = 40
F32 = jnp.float32
BF16 = jnp.bfloat16


def shift(value, axis, by):
    size = lax.axis_size(axis)
    return lax.ppermute(value, axis, [(i, (i + by) % size) for i in range(size)])


def add32(*terms):
    total = terms[0].astype(F32)
    for term in terms[1:]:
        total = total + term.astype(F32)
    return total


CHIPS = ("y", "core")
GROUP = ("y", "zh", "core")
SEQUENCES = ("zl", "x")


def swap(value, axes):
    return lax.all_to_all(value, axes, 0, 0, tiled=True)


def meet(*values):
    return lax.optimization_barrier(values)


def ring_pieces(value):
    return [value, shift(value, "y", -1), shift(value, "y", 2), shift(value, "y", 1)]


def pick(array, index):
    return lax.dynamic_index_in_dim(array, index, 0, keepdims=False)


def join_rows(joined, pieces):
    start = 0
    for piece in pieces:
        joined[start : start + piece.shape[0], :] = piece[...]
        start += piece.shape[0]


def down_product(spots, pieces, act_all):
    count, rows, hidden = act_all.shape
    width = pieces[0].shape[1]
    tile = width // 8
    piece_rows = pieces[0].shape[0]

    def kernel(spots_ref, near_ref, far_ref, act_ref, out_ref, joined, acts):
        @pl.when(pl.program_id(0) == 0)
        def _():
            for i in range(count):
                acts[rows * i : rows * (i + 1), :] = act_ref[spots_ref[i]]

        join_rows(joined, (near_ref, far_ref))
        out_ref[...] = lax.dot_general(
            joined[...], acts[...], (((0,), (0,)), ((), ())), preferred_element_type=F32
        ).astype(BF16)

    return pl.pallas_call(
        kernel,
        grid_spec=pltpu.PrefetchScalarGridSpec(
            num_scalar_prefetch=1,
            grid=(8,),
            in_specs=[pl.BlockSpec((piece_rows, tile), lambda i, s: (0, i))] * 2
            + [pl.BlockSpec((count, rows, hidden), lambda i, s: (0, 0, 0))],
            out_specs=pl.BlockSpec((tile, hidden), lambda i, s: (i, 0)),
            scratch_shapes=[pltpu.VMEM((count * rows, tile), BF16), pltpu.VMEM((count * rows, hidden), BF16)],
        ),
        out_shape=jax.ShapeDtypeStruct((width, hidden), BF16),
        compiler_params=pltpu.CompilerParams(vmem_limit_bytes=60 * 2**20),
        cost_estimate=pl.CostEstimate(
            flops=2 * count * rows * width * hidden, bytes_accessed=16 * 2**20, transcendentals=0
        ),
    )(spots, *pieces, act_all)


def act_product(spots, pieces, w_down):
    rows, held = SLOT_PAD, len(pieces)
    count = sum(p.shape[0] for p in pieces) // rows
    width, hidden = w_down.shape
    steps = 4
    tile = width // steps

    def kernel(spots_ref, *refs):
        w_ref, out_ref, joined, total = refs[held:]
        step = pl.program_id(0)
        join_rows(joined, refs[:held])
        term = jnp.dot(joined[...], w_ref[...], preferred_element_type=F32)

        @pl.when(step == 0)
        def _():
            total[...] = term

        @pl.when(step > 0)
        def _():
            total[...] += term

        @pl.when(step == steps - 1)
        def _():
            for i in range(count):
                out_ref[spots_ref[i]] = total[rows * i : rows * (i + 1), :].astype(BF16)

    return pl.pallas_call(
        kernel,
        grid_spec=pltpu.PrefetchScalarGridSpec(
            num_scalar_prefetch=1,
            grid=(steps,),
            in_specs=[pl.BlockSpec((p.shape[0], tile), lambda i, s: (0, i)) for p in pieces]
            + [pl.BlockSpec((tile, hidden), lambda i, s: (i, 0))],
            out_specs=pl.BlockSpec((count, rows, hidden), lambda i, s: (0, 0, 0)),
            scratch_shapes=[pltpu.VMEM((count * rows, tile), BF16), pltpu.VMEM((count * rows, hidden), F32)],
        ),
        out_shape=jax.ShapeDtypeStruct((count, rows, hidden), BF16),
        compiler_params=pltpu.CompilerParams(vmem_limit_bytes=60 * 2**20),
        cost_estimate=pl.CostEstimate(
            flops=2 * count * rows * width * hidden, bytes_accessed=16 * 2**20, transcendentals=0
        ),
    )(spots, *pieces, w_down)


def over_zl(mine):
    zl = lax.axis_index("zl")
    return add32(pick(mine, zl), *[shift(pick(mine, (zl + e) % 4), "zl", e) for e in (1, 2, 3)])


def attn_product(where, cols_all, out_proj, other_proj):
    _, tokens, both = cols_all.shape
    features, cols = out_proj.shape

    def kernel(where_ref, *refs):
        col_refs, own_ref, other_ref, mine_ref, theirs_ref, joined = refs[:4], *refs[4:]
        for d in range(4):
            joined[tokens * d : tokens * (d + 1), :] = col_refs[d][0]
        near = pl.multiple_of(where_ref[2] * cols, 128)
        far = pl.multiple_of((1 - where_ref[2]) * cols, 128)
        by_cols = (((1,), (1,)), ((), ()))
        product = lax.dot_general(
            joined[:, pl.ds(near, cols)], own_ref[...], by_cols, preferred_element_type=F32
        ) + lax.dot_general(joined[:, pl.ds(far, cols)], other_ref[...], by_cols, preferred_element_type=F32)
        product = product.astype(BF16).reshape(4, tokens, features)

        @pl.when(pl.program_id(0) == 0)
        def _():
            theirs_ref[...] = product

        @pl.when(pl.program_id(0) == 1)
        def _():
            mine_ref[...] = product

    def spot(d):
        return lambda i, s: (((s[0] + d) % 4) * 2 + (s[1] + 1 - i) % 2, 0, 0)

    whole = pl.BlockSpec((features, cols), lambda i, s: (0, 0))
    out = pl.BlockSpec((4, tokens, features), lambda i, s: (0, 0, 0))
    return pl.pallas_call(
        kernel,
        grid_spec=pltpu.PrefetchScalarGridSpec(
            num_scalar_prefetch=1,
            grid=(2,),
            in_specs=[pl.BlockSpec((1, tokens, both), spot(d)) for d in range(4)] + [whole, whole],
            out_specs=[out, out],
            scratch_shapes=[pltpu.VMEM((4 * tokens, both), BF16)],
        ),
        out_shape=[jax.ShapeDtypeStruct((4, tokens, features), BF16)] * 2,
        compiler_params=pltpu.CompilerParams(vmem_limit_bytes=48 * 2**20),
        cost_estimate=pl.CostEstimate(
            flops=16 * tokens * both * features, bytes_accessed=6 * 2**20, transcendentals=0
        ),
    )(where, *[cols_all] * 4, out_proj, other_proj)


def proj_product(where, mine, partner, cols_all):
    _, tokens, features = mine.shape
    both = cols_all.shape[2]

    rows = features // 16

    def kernel(where_ref, mine_ref, partner_ref, cols_ref, *refs):
        outs, (joined, sides, product) = refs[:4], refs[4:]
        for d in range(4):
            row = lax.rem(where_ref[0] + d, 4) * 2
            for f, ref in ((0, mine_ref), (1, partner_ref)):
                start = tokens * (2 * d + f)
                joined[start : start + tokens, :] = ref[d]
                sides[start : start + tokens, :] = cols_ref[row + lax.rem(where_ref[1] + f, 2)]
        product[...] = lax.dot_general(
            joined[...], sides[...], (((0,), (0,)), ((), ())), preferred_element_type=F32
        )
        for d in range(4):
            column = lax.rem(where_ref[3] + d, 4)
            for z in range(4):
                start = pl.multiple_of((4 * z + column) * rows, 16)
                outs[d][z] = product[pl.ds(start, rows), :].astype(BF16)

    piece = pl.BlockSpec((4, rows, both), lambda i, s: (0, 0, 0))
    whole = pl.BlockSpec((4, tokens, features), lambda i, s: (0, 0, 0))
    return pl.pallas_call(
        kernel,
        grid_spec=pltpu.PrefetchScalarGridSpec(
            num_scalar_prefetch=1,
            grid=(1,),
            in_specs=[whole, whole, pl.BlockSpec((8, tokens, both), lambda i, s: (0, 0, 0))],
            out_specs=[piece] * 4,
            scratch_shapes=[
                pltpu.VMEM((8 * tokens, features), BF16),
                pltpu.VMEM((8 * tokens, both), BF16),
                pltpu.VMEM((features, both), F32),
            ],
        ),
        out_shape=[jax.ShapeDtypeStruct((4, rows, both), BF16)] * 4,
        compiler_params=pltpu.CompilerParams(vmem_limit_bytes=48 * 2**20),
        cost_estimate=pl.CostEstimate(
            flops=16 * tokens * both * features, bytes_accessed=6 * 2**20, transcendentals=0
        ),
    )(where, mine, partner, cols_all)


def on_device(grad_out, gates, route_rows, saved_act, queries, keys, values, out_proj, w_down):
    y, zh, core = lax.axis_index("y"), lax.axis_index("zh"), lax.axis_index("core")
    tokens, width = grad_out.shape
    slots = route_rows.shape[0]
    heads = queries.shape[1] // HEAD
    cols = out_proj.shape[1]
    hidden = w_down.shape[1]
    scale = HEAD ** (-0.5)

    kv = jnp.concatenate([keys, values], 1)
    kv_other = shift(kv, "zh", 1)

    rows = jnp.concatenate([route_rows, jnp.full((SLOT_PAD - slots,), tokens, jnp.int32)])
    hot = rows[:, None] == jnp.arange(tokens, dtype=jnp.int32)[None, :]
    picked = jnp.dot(hot.astype(BF16), grad_out, preferred_element_type=F32)
    gate = jnp.sum(jnp.where(hot, gates[None, :], 0.0), axis=1)
    upstream = (gate[:, None] * picked).astype(BF16)

    kv2 = jnp.stack([kv, kv_other])
    kv8 = jnp.stack(ring_pieces(kv2))
    all_kv = jnp.stack([kv8, shift(kv8, "core", 1)]).reshape(16 * tokens, 2 * HEAD)
    all_keys, all_values = all_kv[:, :HEAD], all_kv[:, HEAD:]

    near = lax.all_gather(upstream, CHIPS, axis=0, tiled=True)
    upstream, kv_other = meet(upstream, kv_other)
    other_up = shift(upstream, "zh", 1)

    act_in = jnp.concatenate([saved_act, jnp.zeros((SLOT_PAD - slots, saved_act.shape[1]), BF16)], 0)
    act_in = act_in.reshape(SLOT_PAD, 16, hidden).transpose(1, 0, 2)
    cols_in = grad_out.reshape(tokens, 4, 2, 2, cols).transpose(1, 3, 0, 2, 4).reshape(8, tokens, 2 * cols)
    other_up, out_proj, act_in, cols_in = meet(other_up, out_proj, act_in, cols_in)
    far = lax.all_gather(other_up, CHIPS, axis=0, tiled=True)
    pieces = (near, far)
    spots = jnp.stack(
        [py * 4 + (zh ^ e) * 2 + pc for e in range(2) for py in range(4) for pc in range(2)]
    ).astype(jnp.int32)

    kv2 = jnp.stack([kv, kv_other])
    kv8 = jnp.stack(ring_pieces(kv2))
    all_kv = jnp.stack([kv8, shift(kv8, "core", 1)]).reshape(16 * tokens, 2 * HEAD)
    all_keys, all_values = all_kv[:, :HEAD], all_kv[:, HEAD:]

    place = jnp.arange(16, dtype=jnp.int32)
    block = ((y + (place // 2) % 4) % 4) * 4 + (zh ^ (place % 2)) * 2 + (core ^ (place // 8))
    key_place = (block[:, None] * tokens + jnp.arange(tokens, dtype=jnp.int32)[None, :]).reshape(-1)
    query_place = (y * 4 + zh * 2 + core) * tokens + jnp.arange(tokens, dtype=jnp.int32)

    query3 = queries.reshape(tokens, heads, HEAD)
    scores = jnp.einsum("qhd,kd->hqk", query3, all_keys, preferred_element_type=F32) * scale
    allowed = key_place[None, :] <= query_place[:, None]
    scores = jnp.where(allowed[None], scores, jnp.float32(-1e30))
    highest = jnp.max(scores, axis=2, keepdims=True)
    weights = jnp.exp(scores - highest)
    probs = weights / jnp.sum(weights, axis=2, keepdims=True)
    probs_b = probs.astype(BF16)
    attended = jnp.einsum("hqk,kd->qhd", probs_b, all_values, preferred_element_type=F32).astype(BF16)

    flat = attended.reshape(tokens, heads * HEAD)
    other_proj = shift(out_proj, "zh", 1)
    spots, flat, other_proj = meet(spots, flat, other_proj)
    act_all = swap(act_in, GROUP)
    cols_in, act_all = meet(cols_in, act_all)
    cols_all = swap(cols_in, CHIPS)

    where = jnp.stack([y, core, zh, lax.axis_index("x")]).astype(jnp.int32)
    down = down_product(spots, pieces, act_all)

    spots, where, down = meet(spots, where, down)
    down_grad = lax.psum_scatter(down, SEQUENCES, scatter_dimension=0, tiled=True).astype(F32)

    part = act_product(spots, pieces, w_down)

    att4 = jnp.stack(ring_pieces(flat))
    att_other = shift(att4, "core", 1)
    where, part = meet(where, part)
    mine, theirs = attn_product(where, cols_all, out_proj, other_proj)
    act_back = swap(part, GROUP)
    chip_sum = add32(mine, shift(theirs, "core", 1)).astype(BF16)
    attn_grad = add32(chip_sum[0], *[shift(chip_sum[d], "y", d) for d in (1, 2, 3)]).astype(BF16)

    where, attn_grad = meet(where, attn_grad)
    proj = proj_product(where, att4, att_other, cols_all)

    attn_grad3 = attn_grad.reshape(tokens, heads, HEAD)
    prob_grad = jnp.einsum("qhd,kd->hqk", attn_grad3, all_values, preferred_element_type=F32)
    row_dot = jnp.sum(attn_grad3.astype(F32) * attended.astype(F32), axis=2)
    score_grad = (probs * (prob_grad - row_dot.T[:, :, None])).astype(BF16)
    query_grad = jnp.einsum("hqk,kd->qhd", score_grad, all_keys, preferred_element_type=F32) * scale
    query_grad = query_grad.astype(BF16).reshape(tokens, heads * HEAD)
    key_part = jnp.einsum("hqk,qhd->kd", score_grad, query3, preferred_element_type=F32) * scale
    value_part = jnp.einsum("hqk,qhd->kd", probs_b, attn_grad3, preferred_element_type=F32)
    kv_part = jnp.concatenate([key_part, value_part], axis=1).astype(BF16)
    kv_part = kv_part.reshape(2, 4, 2, tokens, 2 * HEAD)
    kv_chip = add32(kv_part[0], shift(kv_part[1], "core", 1)).astype(BF16)
    kv_ring = add32(kv_chip[0], *[shift(kv_chip[d], "y", d) for d in (1, 2, 3)]).astype(BF16)
    proj = add32(proj[0], *[shift(proj[d], "x", d) for d in (1, 2, 3)]).astype(BF16)
    act_back, proj, kv_ring = meet(act_back, proj, kv_ring)
    act_grad = act_back.transpose(1, 0, 2).reshape(SLOT_PAD, 16 * hidden)[:slots]
    proj = over_zl(proj)
    left, right = proj[:, :cols], proj[:, cols:]
    keep = jnp.where(zh == 0, left, right)
    give = jnp.where(zh == 0, right, left).astype(BF16)
    proj_grad = keep + shift(give, "zh", 1).astype(F32)

    kv_grad = add32(kv_ring[0], shift(kv_ring[1], "zh", 1)).astype(BF16)
    return act_grad, query_grad, kv_grad[:, :HEAD], kv_grad[:, HEAD:], proj_grad, down_grad


def solution(mesh):
    axes = ("zl", "x", "y", "zh", "core")
    fine = Mesh(mesh.devices.reshape(4, 4, 4, 2, 2), axes)
    by_token = P(axes, None)
    by_dev = P(None, ("y", "zh", "core"))
    both = P(("zl", "x"), ("y", "zh", "core"))
    return jax.shard_map(
        on_device,
        mesh=fine,
        in_specs=(by_token, P(axes), P(axes), by_token, by_token, by_token, by_token, by_dev, by_dev),
        out_specs=(by_token, by_token, by_token, by_token, both, both),
        check_vma=False,
    )
```
